32 devices in a mesh: dp: 2 (over x), seq: 4 (over z), tensor: 4 (over y, core).
Axes of the slice: x: 2, y: 2, z: 4, core: 2. Of those that a mesh axis runs over, the one named last changes fastest.
Arguments:
- inputs: bfloat16 [2, 2048, 768], P('dp', ('seq', 'tensor')), may hold values from -6 to 6
- ln1_gain: bfloat16 [768], replicated, may hold values from 0.099609375 to 1.8984375
- ln1_bias: bfloat16 [768], replicated, may hold values from -3 to 3
- w_query: bfloat16 [768, 768], P(None, 'tensor'), may hold values from -0.21875 to 0.21875
- b_query: bfloat16 [768], P('tensor'), may hold values from -3 to 3
- w_key: bfloat16 [768, 768], P(None, 'tensor'), may hold values from -0.21875 to 0.21875
- w_value: bfloat16 [768, 768], P(None, 'tensor'), may hold values from -0.21875 to 0.21875
- b_value: bfloat16 [768], P('tensor'), may hold values from -3 to 3
- w_out: bfloat16 [768, 768], P('tensor'), may hold values from -3.5 to 3.5
- b_out: bfloat16 [768], replicated, may hold values from -1.75 to 1.75
- ln2_gain: bfloat16 [768], replicated, may hold values from 0.099609375 to 1.8984375
- ln2_bias: bfloat16 [768], replicated, may hold values from -3 to 3
- w_up: bfloat16 [768, 3072], P(None, 'tensor'), may hold values from -0.21875 to 0.21875
- b_up: bfloat16 [3072], P('tensor'), may hold values from -3 to 3
- w_down: bfloat16 [3072, 768], P('tensor'), may hold values from -0.109375 to 0.109375
- b_down: bfloat16 [768], replicated, may hold values from -1.75 to 1.75
- cotangent: bfloat16 [2, 2048, 768], P('dp', ('seq', 'tensor')), may hold values from -6 to 6
Outputs:
- output: bfloat16 [2, 2048, 768], P('dp', ('seq', 'tensor'))
- input_grad: bfloat16 [2, 2048, 768], P('dp', ('seq', 'tensor'))
- grad_ln1_gain: float32 [768], P('tensor')
- grad_ln1_bias: float32 [768], P('tensor')
- grad_w_query: float32 [768, 768], P(None, 'tensor')
- grad_b_query: float32 [768], P('tensor')
- grad_w_key: float32 [768, 768], P(None, 'tensor')
- grad_w_value: float32 [768, 768], P(None, 'tensor')
- grad_b_value: float32 [768], P('tensor')
- grad_w_out: float32 [768, 768], P('tensor')
- grad_b_out: float32 [768], P('tensor')
- grad_ln2_gain: float32 [768], P('tensor')
- grad_ln2_bias: float32 [768], P('tensor')
- grad_w_up: float32 [768, 3072], P(None, 'tensor')
- grad_b_up: float32 [3072], P('tensor')
- grad_w_down: float32 [3072, 768], P('tensor')
- grad_b_down: float32 [768], P('tensor')
The draws below stay inside these ranges and needn't reach their ends.
All inputs are finite; a program needn't handle non-finite values.
Results may differ from the reference program's by a relative error of at most 0.01.
The reference program's roundings to bfloat16 on the way count: a program that leaves them out, or rounds other values in their place, can miss the bound.
Values may be sent and summed in bfloat16 or wider, within the bound.
A program may use at most 128 MiB of HBM per device.

```python
import jax
import jax.numpy as jnp
from jax import lax

D = 768
HEADS = 12
HEAD_DIM = 64
FF = 3072
FRAMES = 2048
CLIPS = 2


def levels(stream_key, extent, split, low, largest):
    def one(position, shards_of):
        draws = jax.random.uniform(jax.random.fold_in(jax.random.fold_in(stream_key, 6), position), (shards_of,), jnp.float32, low / len(split), largest / len(split))
        return jnp.repeat(jnp.exp(draws), extent[position] // shards_of).reshape((-1,) + (1,) * (len(extent) - position - 1))

    factor_of = one(*split[0])
    for cut in split[1:]:
        factor_of = factor_of * one(*cut)
    return factor_of


def scatter_about(stream_key, extent, scale, reach, split=(), dtype=jnp.bfloat16):
    entries = scale * jax.random.normal(stream_key, extent, jnp.float32)
    if split:
        entries = entries * levels(stream_key, extent, split, -0.22, 0.18)
    return jnp.clip(entries, -reach, reach).astype(dtype)


def setup_inputs(seed: int = 0) -> dict:
    key_of = jax.random.split(jax.random.key(seed), 18)
    return {
        "inputs": scatter_about(key_of[0], (CLIPS, FRAMES, D), 1.0, 6.0, ((0, 2), (1, 16))),
        "ln1_gain": jnp.clip(1.0 + 0.18 * jax.random.normal(key_of[1], (D,), jnp.float32), 0.099609375, 1.8984375).astype(jnp.bfloat16),
        "ln1_bias": scatter_about(key_of[2], (D,), 0.5, 3.0),
        "w_query": scatter_about(key_of[3], (D, D), D ** -0.5, 0.21875, ((1, 4),)),
        "b_query": scatter_about(key_of[4], (D,), 0.5, 3.0, ((0, 4),)),
        "w_key": scatter_about(key_of[5], (D, D), D ** -0.5, 0.21875, ((1, 4),)),
        "w_value": scatter_about(key_of[6], (D, D), D ** -0.5, 0.21875, ((1, 4),)),
        "b_value": scatter_about(key_of[7], (D,), 0.5, 3.0, ((0, 4),)),
        "w_out": scatter_about(key_of[8], (D, D), (max(D // 256, 1)) ** -0.5, 3.5, ((0, 4),)),
        "b_out": scatter_about(key_of[9], (D,), 0.3, 1.75),
        "ln2_gain": jnp.clip(1.0 + 0.18 * jax.random.normal(key_of[10], (D,), jnp.float32), 0.099609375, 1.8984375).astype(jnp.bfloat16),
        "ln2_bias": scatter_about(key_of[11], (D,), 0.5, 3.0),
        "w_up": scatter_about(key_of[12], (D, FF), D ** -0.5, 0.21875, ((1, 4),)),
        "b_up": scatter_about(key_of[13], (FF,), 0.5, 3.0, ((0, 4),)),
        "w_down": scatter_about(key_of[14], (FF, D), FF ** -0.5, 0.109375, ((0, 4),)),
        "b_down": scatter_about(key_of[15], (D,), 0.3, 1.75),
        "cotangent": scatter_about(key_of[16], (CLIPS, FRAMES, D), 1.0, 6.0, ((0, 2), (1, 16))),
    }


eps = 1e-05

@jax.custom_vjp
def low(v):
    return lax.optimization_barrier(v.astype(jnp.bfloat16)).astype(jnp.float32)

@jax.custom_vjp
def low_back(v):
    return v

def low_keep(v):
    return (low(v), None)

def low_pass(kept, grad):
    return (grad,)

def back_keep(v):
    return (v, None)

def back_low(kept, grad):
    return (low(grad),)
low.defvjp(low_keep, low_pass)
low_back.defvjp(back_keep, back_low)

def matmul(left, right):
    return jnp.dot(left, right, precision=lax.Precision.HIGHEST)

def normalize(values, gain, offset):
    center = values - lax.optimization_barrier(jnp.mean(values, axis=-1, keepdims=True))
    spread = lax.rsqrt(lax.optimization_barrier(jnp.mean(center * center, axis=-1, keepdims=True)) + eps)
    return center * spread * gain + offset

def attend(query, keys, values):
    frames = query.shape[0]
    query3 = query.reshape(frames, HEADS, HEAD_DIM)
    key3 = keys.reshape(frames, HEADS, HEAD_DIM)
    value3 = values.reshape(frames, HEADS, HEAD_DIM)
    scores = low_back(jnp.einsum('qhd,khd->hqk', query3, key3, precision=lax.Precision.HIGHEST) * HEAD_DIM ** (-0.5))
    expo = jnp.exp(scores - lax.optimization_barrier(jnp.max(scores, axis=-1, keepdims=True)))
    probs = low(expo / lax.optimization_barrier(jnp.sum(expo, axis=-1, keepdims=True)))
    mixed = jnp.einsum('hqk,khd->qhd', probs, value3, precision=lax.Precision.HIGHEST)
    return mixed.reshape(frames, HEADS * HEAD_DIM)

def layer(frames_in, params):
    gain_one, shift_one, w_query, b_query, w_key, w_value, b_value, w_out, b_out, gain_two, shift_two, w_up, b_up, w_down, b_down = params
    normed = low(normalize(frames_in, gain_one, shift_one))
    query = low(low_back(matmul(normed, w_query) + b_query))
    keys = low(low_back(matmul(normed, w_key)))
    values = low(low_back(matmul(normed, w_value) + b_value))
    context = low(low_back(jax.checkpoint(attend)(query, keys, values)))
    middle = frames_in + low_back(matmul(context, w_out) + b_out)
    second = low(normalize(middle, gain_two, shift_two))
    hidden = low(jax.nn.gelu(low_back(matmul(second, w_up) + b_up), approximate=False))
    return middle + low_back(matmul(hidden, w_down) + b_down)

def reference(inputs, ln1_gain, ln1_bias, w_query, b_query, w_key, w_value, b_value, w_out, b_out, ln2_gain, ln2_bias, w_up, b_up, w_down, b_down, cotangent):
    params = tuple((p.astype(jnp.float32) for p in (ln1_gain, ln1_bias, w_query, b_query, w_key, w_value, b_value, w_out, b_out, ln2_gain, ln2_bias, w_up, b_up, w_down, b_down)))

    def per_clip(totals, pair):
        clip, upstream = pair
        result, pull = jax.vjp(layer, clip, params)
        grad_clip, grad_params = pull(upstream)
        return (jax.tree.map(jnp.add, totals, grad_params), (result, grad_clip))
    zeros = jax.tree.map(jnp.zeros_like, params)
    totals, (results, grads_in) = lax.scan(per_clip, zeros, (inputs.astype(jnp.float32), cotangent.astype(jnp.float32)))
    return (results.astype(jnp.bfloat16), grads_in.astype(jnp.bfloat16), totals[0], totals[1], totals[2], totals[3], totals[4], totals[5], totals[6], totals[7], totals[8], totals[9], totals[10], totals[11], totals[12], totals[13], totals[14])
```

```python
from functools import partial

import jax
import jax.numpy as jnp
import numpy as np
from jax import lax
from jax.sharding import PartitionSpec as P

HEAD_DIM = 64


eps = 1e-05


def product(left, right):
    return jnp.dot(left, right, preferred_element_type=jnp.float32)


def product_rows(left, right):
    return lax.dot_general(
        left, right, (((0,), (0,)), ((), ())), preferred_element_type=jnp.float32
    )


def product_cols(left, right):
    return lax.dot_general(
        left, right, (((1,), (1,)), ((), ())), preferred_element_type=jnp.float32
    )


def normalize(values, gain, offset):
    center = values - jnp.mean(values, axis=-1, keepdims=True)
    spread = lax.rsqrt(jnp.mean(center * center, axis=-1, keepdims=True) + eps)
    scaled = center * spread
    return (scaled * gain + offset, scaled, spread)


def normalize_back(upstream, scaled, spread, gain):
    inner = upstream * gain
    return spread * (
        inner
        - jnp.mean(inner, axis=-1, keepdims=True)
        - scaled * jnp.mean(inner * scaled, axis=-1, keepdims=True)
    )


def own_columns(vector, rank, share):
    return lax.dynamic_slice_in_dim(vector, rank * share, share, 0)


def scatter(terms):
    return lax.psum_scatter(
        terms.astype(jnp.bfloat16), "tensor", scatter_dimension=0, tiled=True
    )


def local(
    inputs,
    ln1_gain,
    ln1_bias,
    w_query,
    b_query,
    w_key,
    w_value,
    b_value,
    w_out,
    b_out,
    ln2_gain,
    ln2_bias,
    w_up,
    b_up,
    w_down,
    b_down,
    cotangent,
):
    f32, bf16 = jnp.float32, jnp.bfloat16
    own_rows, width = inputs.shape[1:]
    lanes = lax.axis_size("tensor")
    rank = lax.axis_index("tensor")
    share = width // lanes
    gain_one = ln1_gain.astype(f32)
    gain_two = ln2_gain.astype(f32)
    frames_in = inputs[0].astype(f32)
    both = lax.all_gather(
        jnp.concatenate([inputs[0], cotangent[0]], axis=1), "tensor", axis=0, tiled=True
    )
    grad_z_all = both[:, width:]
    normed_one, scaled_all, _ = normalize(
        both[:, :width].astype(f32), gain_one, ln1_bias.astype(f32)
    )
    attn_input = normed_one.astype(bf16)
    heads_width = w_query.shape[1]
    keys = product(attn_input, w_key).astype(bf16)
    values = (product(attn_input, w_value) + b_value.astype(f32)).astype(bf16)
    kv_all = lax.all_gather(jnp.concatenate([keys, values], axis=1), "seq", axis=0, tiled=True)
    query = (product(attn_input, w_query) + b_query.astype(f32)).astype(bf16)
    grad_hidden = product_cols(grad_z_all, w_down)
    frames = query.shape[0]
    heads = heads_width // HEAD_DIM
    scale = HEAD_DIM ** (-0.5)
    query3 = query.reshape(frames, heads, HEAD_DIM)
    key3 = kv_all[:, :heads_width].reshape(kv_all.shape[0], heads, HEAD_DIM)
    value3 = kv_all[:, heads_width:].reshape(kv_all.shape[0], heads, HEAD_DIM)
    scores = jnp.einsum("qhd,khd->hqk", query3, key3, preferred_element_type=f32) * scale
    top = jnp.max(scores, axis=-1, keepdims=True)
    expo = jnp.exp(scores - top)
    total = jnp.sum(expo, axis=-1, keepdims=True)
    logsum = top + jnp.log(total)
    weights_low = (expo / total).astype(bf16)
    context = jnp.einsum("hqk,khd->qhd", weights_low, value3, preferred_element_type=f32)
    context = context.reshape(frames, heads_width).astype(bf16)
    attn_rows = scatter(product(context, w_out)).astype(f32)
    middle = frames_in + attn_rows + b_out.astype(f32)
    normed_two, scaled_two, spread_two = normalize(middle, gain_two, ln2_bias.astype(f32))
    mlp_input = lax.all_gather(normed_two.astype(bf16), "tensor", axis=0, tiled=True)
    before = product(mlp_input, w_up) + b_up.astype(f32)
    activated, gelu_back = jax.vjp(partial(jax.nn.gelu, approximate=False), before)
    hidden = activated.astype(bf16)
    (grad_before,) = gelu_back(grad_hidden)
    grad_before = grad_before.astype(bf16)
    grad_two = scatter(product_cols(grad_before, w_up)).astype(f32)
    upstream = cotangent[0].astype(f32)
    grad_middle = upstream + normalize_back(grad_two, scaled_two, spread_two, gain_two)
    grad_attn_rows = grad_middle.astype(bf16)
    sums_two = jnp.stack([jnp.sum(grad_two * scaled_two, axis=0), jnp.sum(grad_two, axis=0)])
    high = sums_two.astype(bf16)
    low = (sums_two - high.astype(f32)).astype(bf16)
    extra = jnp.concatenate([high, low, jnp.zeros((12, width), bf16)])
    packed = lax.all_gather(jnp.concatenate([grad_attn_rows, extra]), "tensor", axis=0)
    grad_attn_all = packed[:, :own_rows].reshape(frames, width)
    pair = packed[:, own_rows : own_rows + 4].astype(f32).sum(axis=0)
    pair = lax.dynamic_slice_in_dim(pair[:2] + pair[2:], rank * share, share, 1)
    mlp_rows = scatter(product(hidden, w_down)).astype(f32)
    result = (middle + mlp_rows + b_down.astype(f32)).astype(bf16)
    grad_down = product_rows(hidden, grad_z_all)
    grad_up = product_rows(mlp_input, grad_before)
    grad_wout = product_rows(context, grad_attn_all)
    early = lax.psum(
        (grad_up.astype(bf16), grad_down.astype(bf16), grad_wout.astype(bf16)), ("dp", "seq")
    )
    grad_context = (
        product_cols(grad_attn_all, w_out).astype(bf16).reshape(frames, heads, HEAD_DIM)
    )
    scores_again = jnp.einsum("qhd,khd->hqk", query3, key3, preferred_element_type=f32) * scale
    probs = jnp.exp(scores_again - logsum)
    probs_low = probs.astype(bf16)
    grad_probs = jnp.einsum("qhd,khd->hqk", grad_context, value3, preferred_element_type=f32)
    inner_sum = jnp.sum(probs * grad_probs, axis=-1, keepdims=True)
    grad_scores = (probs * (grad_probs - inner_sum)).astype(bf16)
    key_terms = jnp.einsum("hqk,qhd->khd", grad_scores, query3, preferred_element_type=f32) * scale
    key_terms = key_terms.reshape(kv_all.shape[0], heads_width)
    value_terms = jnp.einsum("hqk,qhd->khd", probs_low, grad_context, preferred_element_type=f32)
    value_terms = value_terms.reshape(kv_all.shape[0], heads_width)
    grad_kv = lax.psum_scatter(
        jnp.concatenate([key_terms, value_terms], axis=1).astype(bf16),
        "seq",
        scatter_dimension=0,
        tiled=True,
    )
    grad_query = jnp.einsum("hqk,khd->qhd", grad_scores, key3, preferred_element_type=f32) * scale
    grad_query = grad_query.reshape(frames, heads_width).astype(bf16)
    grad_keys = grad_kv[:, :heads_width]
    grad_values = grad_kv[:, heads_width:]
    term = (
        product_cols(grad_query, w_query)
        + product_cols(grad_keys, w_key)
        + product_cols(grad_values, w_value)
    )
    grad_one = scatter(term).astype(f32)
    grad_qkv = product_rows(attn_input, jnp.concatenate([grad_query, grad_kv], axis=1))
    grad_qkv, early = lax.optimization_barrier((grad_qkv.astype(bf16), early))
    late = lax.psum(grad_qkv, ("dp", "seq")).astype(f32)
    scaled_one, spread_one = normalize(frames_in, gain_one, ln1_bias.astype(f32))[1:]
    grad_input = (grad_middle + normalize_back(grad_one, scaled_one, spread_one, gain_one)).astype(
        bf16
    )
    sums_one = jnp.concatenate([jnp.sum(term * scaled_all, axis=0), jnp.sum(term, axis=0)])
    sums_one = lax.all_gather(sums_one.reshape(-1, share), "tensor", axis=0)
    sums_one = sums_one.sum(axis=0).reshape(2, lanes, share)
    sums_one = lax.dynamic_index_in_dim(sums_one, rank, 1, keepdims=False)
    mine = [
        sums_one[0],
        sums_one[1],
        jnp.sum(grad_query.astype(f32), axis=0),
        jnp.sum(grad_values.astype(f32), axis=0),
        own_columns(jnp.sum(grad_attn_all.astype(f32), axis=0), rank, share),
        pair[0],
        pair[1],
        own_columns(jnp.sum(grad_z_all.astype(f32), axis=0), rank, share),
        jnp.sum(grad_before.astype(f32), axis=0),
    ]
    ends = np.cumsum([part.shape[0] for part in mine])[:-1]
    totals = lax.all_gather(jnp.concatenate(mine)[None], ("dp", "seq"), axis=0).sum(axis=(0, 1))
    gain1, bias1, bq, bv, bo, gain2, bias2, bd, bu = jnp.split(totals, ends)
    return (
        result[None],
        grad_input[None],
        gain1,
        bias1,
        late[:, :heads_width],
        bq,
        late[:, heads_width : 2 * heads_width],
        late[:, 2 * heads_width :],
        bv,
        early[2].astype(f32),
        bo,
        gain2,
        bias2,
        early[0].astype(f32),
        bu,
        early[1].astype(f32),
        bd,
    )


def solution(mesh):
    placed = (
        P("dp", ("seq", "tensor"), None),
        P(),
        P(),
        P(None, "tensor"),
        P("tensor"),
        P(None, "tensor"),
        P(None, "tensor"),
        P("tensor"),
        P("tensor", None),
        P(),
        P(),
        P(),
        P(None, "tensor"),
        P("tensor"),
        P("tensor", None),
        P(),
        P("dp", ("seq", "tensor"), None),
    )
    return jax.shard_map(
        local,
        mesh=mesh,
        in_specs=placed,
        out_specs=(
            P("dp", ("seq", "tensor"), None),
            P("dp", ("seq", "tensor"), None),
            P("tensor"),
            P("tensor"),
            P(None, "tensor"),
            P("tensor"),
            P(None, "tensor"),
            P(None, "tensor"),
            P("tensor"),
            P("tensor", None),
            P("tensor"),
            P("tensor"),
            P("tensor"),
            P(None, "tensor"),
            P("tensor"),
            P("tensor", None),
            P("tensor"),
        ),
        check_vma=False,
    )
```

```python
from functools import partial

import jax
import jax.numpy as jnp
import numpy as np
from jax import lax
from jax.experimental import pallas as pl
from jax.experimental.pallas import tpu as pltpu
from jax.sharding import PartitionSpec as P

HEAD_DIM = 64


eps = 1e-05


def product(left, right):
    return jnp.dot(left, right, preferred_element_type=jnp.float32)


def product_rows(left, right):
    return lax.dot_general(
        left, right, (((0,), (0,)), ((), ())), preferred_element_type=jnp.float32
    )


def product_cols(left, right):
    return lax.dot_general(
        left, right, (((1,), (1,)), ((), ())), preferred_element_type=jnp.float32
    )


def normalize(values, gain, offset):
    center = values - jnp.mean(values, axis=-1, keepdims=True)
    spread = lax.rsqrt(jnp.mean(center * center, axis=-1, keepdims=True) + eps)
    scaled = center * spread
    return (scaled * gain + offset, scaled, spread)


def normalize_back(upstream, scaled, spread, gain):
    inner = upstream * gain
    return spread * (
        inner
        - jnp.mean(inner, axis=-1, keepdims=True)
        - scaled * jnp.mean(inner * scaled, axis=-1, keepdims=True)
    )


def own_columns(vector, rank, share):
    return lax.dynamic_slice_in_dim(vector, rank * share, share, 0)


def as_rows(values, multiple):
    pad = -values.shape[-1] % (128 * multiple)
    values = jnp.pad(values, [(0, 0)] * (values.ndim - 1) + [(0, pad)])
    return values.reshape(*values.shape[:-1], -1, 128)


def call(kernel, number, out_shape, scratch, bytes_moved, *operands):
    vmem = pl.BlockSpec(memory_space=pltpu.VMEM)
    return pl.pallas_call(
        kernel,
        out_shape=out_shape,
        in_specs=[vmem] * len(operands),
        out_specs=jax.tree.map(lambda _: vmem, out_shape),
        scratch_shapes=scratch,
        compiler_params=pltpu.CompilerParams(
            collective_id=number, has_side_effects=True, vmem_limit_bytes=40 * 2**20
        ),
        cost_estimate=pl.CostEstimate(flops=0, bytes_accessed=bytes_moved, transcendentals=0),
    )(*operands)


def greet(peers):
    barrier = pltpu.get_barrier_semaphore()
    for peer in peers:
        pl.semaphore_signal(barrier, inc=1, device_id=peer, device_id_type=pl.DeviceIdType.MESH)
    pl.semaphore_wait(barrier, len(peers))


def send(source, target, sems, slot, peer):
    return pltpu.make_async_remote_copy(
        src_ref=source,
        dst_ref=target,
        send_sem=sems[0].at[slot],
        recv_sem=sems[1].at[slot],
        device_id=peer,
        device_id_type=pl.DeviceIdType.MESH,
    )


def peers_along(axis, n):
    me = lax.axis_index(axis)
    return [{axis: lax.rem(me + step, n)} for step in range(1, n)]


def block(ref, index, rows):
    return ref.at[pl.ds(pl.multiple_of(index * rows, 16), rows)]


def gather_kernel(n, x, out, *sems):
    rows = x.shape[0]
    me = lax.axis_index("tensor")
    peers = peers_along("tensor", n)
    greet(peers)
    copies = [
        send(x, block(out, me, rows), sems, step, peer) for step, peer in enumerate(peers)
    ]
    for copy in copies:
        copy.start()
    block(out, me, rows)[...] = x[...]
    for copy in copies:
        copy.wait()


def gather(x, number):
    n = lax.axis_size("tensor")
    shape = jax.ShapeDtypeStruct((n * x.shape[0], x.shape[1]), x.dtype)
    sems = [pltpu.SemaphoreType.DMA((n - 1,))] * 2
    return call(partial(gather_kernel, n), number, shape, sems, 2**24, x)


def scatter_start(n, x, held, sems, peers):
    rows = x.shape[0] // n
    me = lax.axis_index("tensor")
    copies = [
        send(block(x, lax.rem(me + step + 1, n), rows), held.at[step], sems, step, peer)
        for step, peer in enumerate(peers)
    ]
    for copy in copies:
        copy.start()
    return copies


def scatter_end(n, x, out, held, copies):
    rows = x.shape[0] // n
    total = block(x, lax.axis_index("tensor"), rows)[...].astype(jnp.float32)
    for step, copy in enumerate(copies):
        copy.wait_recv()
        total += held[step].astype(jnp.float32)
    out[...] = total
    for copy in copies:
        copy.wait_send()


def scatter_kernel(n, x, out, held, *sems):
    peers = peers_along("tensor", n)
    greet(peers)
    scatter_end(n, x, out, held, scatter_start(n, x, held, sems, peers))


def scatter(terms, number):
    n = lax.axis_size("tensor")
    rows, width = terms.shape[0] // n, terms.shape[1]
    return call(
        partial(scatter_kernel, n),
        number,
        jax.ShapeDtypeStruct((rows, width), jnp.float32),
        [pltpu.VMEM((n - 1, rows, width), jnp.bfloat16)] + [pltpu.SemaphoreType.DMA((n - 1,))] * 2,
        2**24,
        terms.astype(jnp.bfloat16),
    )


def line_gather_kernel(n, x, out, *sems):
    rows = x.shape[0]
    me = lax.axis_index("seq")
    greet(peers_along("seq", n))
    right, left = {"seq": lax.rem(me + 1, n)}, {"seq": lax.rem(me + n - 1, n)}
    block(out, me, rows)[...] = x[...]

    def hop(step, side):
        owner = lax.rem(me + (n - step if side == 0 else step), n)
        here = block(out, owner, rows)
        return send(here, here, sems[2 * side : 2 * side + 2], step, (right, left)[side])

    for step in range(n - 1):
        pl.when((me >= step) & (me < n - 1))(lambda: hop(step, 0).start())
        pl.when((me + step < n) & (me > 0))(lambda: hop(step, 1).start())
        pl.when(me > step)(lambda: hop(step, 0).wait_recv())
        pl.when(me + step + 1 < n)(lambda: hop(step, 1).wait_recv())
    for step in range(n - 1):
        pl.when((me >= step) & (me < n - 1))(lambda: hop(step, 0).wait_send())
        pl.when((me + step < n) & (me > 0))(lambda: hop(step, 1).wait_send())


def line_gather(x, number):
    n = lax.axis_size("seq")
    shape = jax.ShapeDtypeStruct((n * x.shape[0], x.shape[1]), x.dtype)
    sems = [pltpu.SemaphoreType.DMA((n - 1,))] * 4
    return call(partial(line_gather_kernel, n), number, shape, sems, 2**25, x)


def line_scatter_kernel(n, x, out, held, staged, *sems):
    rows = x.shape[0] // n
    me = lax.axis_index("seq")
    greet(peers_along("seq", n))
    neighbours = {"seq": lax.rem(me + 1, n)}, {"seq": lax.rem(me + n - 1, n)}

    def hop(step, side):
        return send(
            staged.at[side, step],
            held.at[side, step],
            sems[2 * side : 2 * side + 2],
            step,
            neighbours[side],
        )

    def advance(step, side):
        place = me if side == 0 else n - 1 - me
        mine = x[pl.ds((n - 1 - step if side == 0 else step) * rows, rows), :]

        def first():
            staged[side, step] = mine
            hop(step, side).start()

        def later():
            passing = held[side, step].astype(jnp.float32)
            staged[side, step] = (mine.astype(jnp.float32) + passing).astype(mine.dtype)
            hop(step, side).start()

        pl.when((place > 0) & (place <= n - 1 - step))(lambda: hop(step, side).wait_recv())
        pl.when(place == 0)(first)
        pl.when((place > 0) & (place < n - 1 - step))(later)

    for step in range(n - 1):
        advance(step, 0)
        advance(step, 1)
    out[...] = block(x, me, rows)[...].astype(jnp.float32)

    def add(side, step):
        out[...] += held[side, step].astype(jnp.float32)

    for step in range(n - 1):
        pl.when(me == n - 1 - step)(lambda: add(0, step))
        pl.when(me == step)(lambda: add(1, step))
    for step in range(n - 1):
        pl.when(me < n - 1 - step)(lambda: hop(step, 0).wait_send())
        pl.when(n - 1 - me < n - 1 - step)(lambda: hop(step, 1).wait_send())


def line_scatter(x, number):
    n = lax.axis_size("seq")
    rows, width = x.shape[0] // n, x.shape[1]
    return call(
        partial(line_scatter_kernel, n),
        number,
        jax.ShapeDtypeStruct((rows, width), jnp.float32),
        [pltpu.VMEM((2, n - 1, rows, width), x.dtype)] * 2
        + [pltpu.SemaphoreType.DMA((n - 1,))] * 4,
        2**25,
        x,
    )


def final_kernel(
    n,
    dp,
    seq,
    term,
    mlp,
    w,
    v_one,
    v_two,
    term_out,
    mlp_out,
    w_out,
    v_out,
    term_held,
    mlp_held,
    w_held,
    w_total,
    v_one_held,
    v_mine,
    v_held,
    *sems,
):
    f32 = jnp.float32
    count = dp * seq
    rows = w.shape[0] // count
    lane = lax.axis_index("tensor")
    me = lax.axis_index("dp") * seq + lax.axis_index("seq")
    near = peers_along("tensor", n)

    def far(step):
        index = lax.rem(me + step, count)
        return index, {"dp": index // seq, "seq": lax.rem(index, seq)}

    barrier = pltpu.get_barrier_semaphore()

    def signal(peer):
        pl.semaphore_signal(barrier, inc=1, device_id=peer, device_id_type=pl.DeviceIdType.MESH)

    for peer in near:
        signal(peer)
    pl.loop(1, count)(lambda step: signal(far(step)[1]))
    pl.semaphore_wait(barrier, n - 1 + count - 1)

    pairs = [sems[i : i + 2] for i in range(0, len(sems), 2)]
    ones = [
        send(v_one.at[lax.rem(lane + step + 1, n)], v_one_held.at[step], pairs[0], step, peer)
        for step, peer in enumerate(near)
    ]
    for copy in ones:
        copy.start()

    def first(step):
        index, peer = far(step)
        return send(block(w, index, rows), w_held.at[step - 1], pairs[1], step - 1, peer)

    def second(step):
        here = block(w_out, me, rows)
        return send(here, here, pairs[2], step - 1, far(step)[1])

    def vector(step):
        return send(v_mine, v_held.at[step - 1], pairs[3], step - 1, far(step)[1])

    pl.loop(1, count)(lambda step: first(step).start())
    terms = scatter_start(n, term, term_held, pairs[4], near)
    mlps = scatter_start(n, mlp, mlp_held, pairs[5], near)
    total = v_one[lane]
    for step, copy in enumerate(ones):
        copy.wait_recv()
        total += v_one_held[step]
    v_mine[0:8, :] = total
    v_mine[8:, :] = v_two[...]
    pl.loop(1, count)(lambda step: vector(step).start())
    w_total[...] = block(w, me, rows)[...].astype(f32)

    @pl.loop(1, count)
    def _(step):
        first(step).wait_recv()
        w_total[...] += w_held[step - 1].astype(f32)

    block(w_out, me, rows)[...] = w_total[...].astype(w_out.dtype)
    pl.loop(1, count)(lambda step: second(step).start())
    scatter_end(n, term, term_out, term_held, terms)
    scatter_end(n, mlp, mlp_out, mlp_held, mlps)
    v_out[...] = v_mine[...]

    @pl.loop(1, count)
    def _(step):
        vector(step).wait_recv()
        v_out[...] += v_held[step - 1]

    for copy in ones:
        copy.wait_send()

    @pl.loop(1, count)
    def _(step):
        second(step).wait_recv()
        first(step).wait_send()
        second(step).wait_send()
        vector(step).wait_send()


def final(term, mlp, w, v_one, v_two, number):
    n, dp, seq = lax.axis_size("tensor"), lax.axis_size("dp"), lax.axis_size("seq")
    f32, bf16 = jnp.float32, jnp.bfloat16
    count = dp * seq
    pad = -w.shape[0] % (16 * count)
    w = jnp.pad(w, ((0, pad), (0, 0))) if pad else w
    rows = term.shape[0] // n
    vectors = (8 + v_two.shape[0], 128)
    part = w.shape[0] // count
    held = pltpu.VMEM((n - 1, rows, term.shape[1]), bf16)
    near, far = [pltpu.SemaphoreType.DMA((n - 1,))] * 2, [pltpu.SemaphoreType.DMA((count - 1,))] * 2
    return call(
        partial(final_kernel, n, dp, seq),
        number,
        (
            jax.ShapeDtypeStruct((rows, term.shape[1]), f32),
            jax.ShapeDtypeStruct((rows, term.shape[1]), f32),
            jax.ShapeDtypeStruct(w.shape, bf16),
            jax.ShapeDtypeStruct(vectors, f32),
        ),
        [
            held,
            held,
            pltpu.VMEM((count - 1, part, w.shape[1]), bf16),
            pltpu.VMEM((part, w.shape[1]), f32),
            pltpu.VMEM((n - 1, 8, 128), f32),
            pltpu.VMEM(vectors, f32),
            pltpu.VMEM((count - 1, *vectors), f32),
        ]
        + near
        + far * 3
        + near * 2,
        2**26,
        term,
        mlp,
        w,
        v_one,
        v_two,
    )


def local(
    inputs,
    ln1_gain,
    ln1_bias,
    w_query,
    b_query,
    w_key,
    w_value,
    b_value,
    w_out,
    b_out,
    ln2_gain,
    ln2_bias,
    w_up,
    b_up,
    w_down,
    b_down,
    cotangent,
):
    f32, bf16 = jnp.float32, jnp.bfloat16
    own_rows, width = inputs.shape[1:]
    lanes = lax.axis_size("tensor")
    rank = lax.axis_index("tensor")
    share = width // lanes
    gain_one = ln1_gain.astype(f32)
    gain_two = ln2_gain.astype(f32)
    frames_in = inputs[0].astype(f32)
    both = gather(jnp.concatenate([inputs[0], cotangent[0]], axis=1), 1)
    grad_z_all = both[:, width:]
    normed_one, scaled_all, _ = normalize(
        both[:, :width].astype(f32), gain_one, ln1_bias.astype(f32)
    )
    attn_input = normed_one.astype(bf16)
    heads_width = w_query.shape[1]
    keys = product(attn_input, w_key).astype(bf16)
    values = (product(attn_input, w_value) + b_value.astype(f32)).astype(bf16)
    kv_all = line_gather(jnp.concatenate([keys, values], axis=1), 2)
    query = (product(attn_input, w_query) + b_query.astype(f32)).astype(bf16)
    grad_hidden = product_cols(grad_z_all, w_down)
    frames = query.shape[0]
    heads = heads_width // HEAD_DIM
    scale = HEAD_DIM ** (-0.5)
    query3 = query.reshape(frames, heads, HEAD_DIM)
    key3 = kv_all[:, :heads_width].reshape(kv_all.shape[0], heads, HEAD_DIM)
    value3 = kv_all[:, heads_width:].reshape(kv_all.shape[0], heads, HEAD_DIM)
    scores = jnp.einsum("qhd,khd->hqk", query3, key3, preferred_element_type=f32) * scale
    top = jnp.max(scores, axis=-1, keepdims=True)
    expo = jnp.exp(scores - top)
    total = jnp.sum(expo, axis=-1, keepdims=True)
    logsum = top + jnp.log(total)
    weights_low = (expo / total).astype(bf16)
    context = jnp.einsum("hqk,khd->qhd", weights_low, value3, preferred_element_type=f32)
    context = context.reshape(frames, heads_width).astype(bf16)
    attn_rows = scatter(product(context, w_out), 3)
    middle = frames_in + attn_rows + b_out.astype(f32)
    normed_two, scaled_two, spread_two = normalize(middle, gain_two, ln2_bias.astype(f32))
    mlp_input = gather(normed_two.astype(bf16), 4)
    before = product(mlp_input, w_up) + b_up.astype(f32)
    activated, gelu_back = jax.vjp(partial(jax.nn.gelu, approximate=False), before)
    hidden = activated.astype(bf16)
    (grad_before,) = gelu_back(grad_hidden)
    grad_before = grad_before.astype(bf16)
    grad_two = scatter(product_cols(grad_before, w_up), 5)
    upstream = cotangent[0].astype(f32)
    grad_middle = upstream + normalize_back(grad_two, scaled_two, spread_two, gain_two)
    grad_attn_rows = grad_middle.astype(bf16)
    sums_two = jnp.stack([jnp.sum(grad_two * scaled_two, axis=0), jnp.sum(grad_two, axis=0)])
    high = sums_two.astype(bf16)
    low = (sums_two - high.astype(f32)).astype(bf16)
    extra = jnp.concatenate([high, low, jnp.zeros((12, width), bf16)])
    packed = gather(jnp.concatenate([grad_attn_rows, extra]), 6).reshape(lanes, -1, width)
    grad_attn_all = packed[:, :own_rows].reshape(frames, width)
    pair = packed[:, own_rows : own_rows + 4].astype(f32).sum(axis=0)
    pair = lax.dynamic_slice_in_dim(pair[:2] + pair[2:], rank * share, share, 1)
    mlp_terms = product(hidden, w_down).astype(bf16)
    grad_down = product_rows(hidden, grad_z_all)
    grad_up = product_rows(mlp_input, grad_before)
    grad_wout = product_rows(context, grad_attn_all)
    early = lax.psum((grad_up.astype(bf16), grad_down.astype(bf16)), ("dp", "seq"))
    grad_wout, early = lax.optimization_barrier((grad_wout.astype(bf16), early))
    sum_wout = lax.psum(grad_wout, ("dp", "seq"))
    grad_context = (
        product_cols(grad_attn_all, w_out).astype(bf16).reshape(frames, heads, HEAD_DIM)
    )
    scores_again = jnp.einsum("qhd,khd->hqk", query3, key3, preferred_element_type=f32) * scale
    probs = jnp.exp(scores_again - logsum)
    probs_low = probs.astype(bf16)
    grad_probs = jnp.einsum("qhd,khd->hqk", grad_context, value3, preferred_element_type=f32)
    inner_sum = jnp.sum(probs * grad_probs, axis=-1, keepdims=True)
    grad_scores = (probs * (grad_probs - inner_sum)).astype(bf16)
    key_terms = jnp.einsum("hqk,qhd->khd", grad_scores, query3, preferred_element_type=f32) * scale
    key_terms = key_terms.reshape(kv_all.shape[0], heads_width)
    value_terms = jnp.einsum("hqk,qhd->khd", probs_low, grad_context, preferred_element_type=f32)
    value_terms = value_terms.reshape(kv_all.shape[0], heads_width)
    grad_kv = line_scatter(
        jnp.concatenate([key_terms, value_terms], axis=1).astype(bf16), 7
    ).astype(bf16)
    grad_query = jnp.einsum("hqk,khd->qhd", grad_scores, key3, preferred_element_type=f32) * scale
    grad_query = grad_query.reshape(frames, heads_width).astype(bf16)
    grad_keys = grad_kv[:, :heads_width]
    grad_values = grad_kv[:, heads_width:]
    term = (
        product_cols(grad_query, w_query)
        + product_cols(grad_keys, w_key)
        + product_cols(grad_values, w_value)
    )
    grad_qkv = product_rows(attn_input, jnp.concatenate([grad_query, grad_kv], axis=1))
    sums_one = jnp.stack([jnp.sum(term * scaled_all, axis=0), jnp.sum(term, axis=0)])
    v_one = sums_one.reshape(2, lanes, share).swapaxes(0, 1).reshape(lanes, -1)
    v_one = as_rows(v_one, 8)
    mine = [
        jnp.sum(grad_query.astype(f32), axis=0),
        jnp.sum(grad_values.astype(f32), axis=0),
        own_columns(jnp.sum(grad_attn_all.astype(f32), axis=0), rank, share),
        pair[0],
        pair[1],
        own_columns(jnp.sum(grad_z_all.astype(f32), axis=0), rank, share),
        jnp.sum(grad_before.astype(f32), axis=0),
    ]
    ends = np.cumsum([part.shape[0] for part in mine])
    grad_one, mlp_rows, late, totals = final(
        term.astype(bf16),
        mlp_terms,
        grad_qkv.astype(bf16),
        v_one,
        as_rows(jnp.concatenate(mine), 16),
        8,
    )
    result = (middle + mlp_rows + b_down.astype(f32)).astype(bf16)
    late = late[:width].astype(f32)
    gain1, bias1 = totals[:8].reshape(-1)[: 2 * share].reshape(2, share)
    bq, bv, bo, gain2, bias2, bd, bu = jnp.split(totals[8:].reshape(-1)[: ends[-1]], ends[:-1])
    scaled_one, spread_one = normalize(frames_in, gain_one, ln1_bias.astype(f32))[1:]
    grad_input = (grad_middle + normalize_back(grad_one, scaled_one, spread_one, gain_one)).astype(
        bf16
    )
    return (
        result[None],
        grad_input[None],
        gain1,
        bias1,
        late[:, :heads_width],
        bq,
        late[:, heads_width : 2 * heads_width],
        late[:, 2 * heads_width :],
        bv,
        sum_wout.astype(f32),
        bo,
        gain2,
        bias2,
        early[0].astype(f32),
        bu,
        early[1].astype(f32),
        bd,
    )


def solution(mesh):
    placed = (
        P("dp", ("seq", "tensor"), None),
        P(),
        P(),
        P(None, "tensor"),
        P("tensor"),
        P(None, "tensor"),
        P(None, "tensor"),
        P("tensor"),
        P("tensor", None),
        P(),
        P(),
        P(),
        P(None, "tensor"),
        P("tensor"),
        P("tensor", None),
        P(),
        P("dp", ("seq", "tensor"), None),
    )
    return jax.shard_map(
        local,
        mesh=mesh,
        in_specs=placed,
        out_specs=(
            P("dp", ("seq", "tensor"), None),
            P("dp", ("seq", "tensor"), None),
            P("tensor"),
            P("tensor"),
            P(None, "tensor"),
            P("tensor"),
            P(None, "tensor"),
            P(None, "tensor"),
            P("tensor"),
            P("tensor", None),
            P("tensor"),
            P("tensor"),
            P("tensor"),
            P(None, "tensor"),
            P("tensor"),
            P("tensor", None),
            P("tensor"),
        ),
        check_vma=False,
    )
```

```python
from functools import partial

import jax
import jax.numpy as jnp
import numpy as np
from jax import lax
from jax.experimental import pallas as pl
from jax.experimental.pallas import tpu as pltpu
from jax.sharding import PartitionSpec as P

HEAD_DIM = 64


eps = 1e-05


def product(left, right):
    return jnp.dot(left, right, preferred_element_type=jnp.float32)


def product_rows(left, right):
    return lax.dot_general(
        left, right, (((0,), (0,)), ((), ())), preferred_element_type=jnp.float32
    )


def product_cols(left, right):
    return lax.dot_general(
        left, right, (((1,), (1,)), ((), ())), preferred_element_type=jnp.float32
    )


def normalize(values, gain, offset):
    center = values - jnp.mean(values, axis=-1, keepdims=True)
    spread = lax.rsqrt(jnp.mean(center * center, axis=-1, keepdims=True) + eps)
    scaled = center * spread
    return (scaled * gain + offset, scaled, spread)


def normalize_back(upstream, scaled, spread, gain):
    inner = upstream * gain
    return spread * (
        inner
        - jnp.mean(inner, axis=-1, keepdims=True)
        - scaled * jnp.mean(inner * scaled, axis=-1, keepdims=True)
    )


def own_columns(vector, rank, share):
    return lax.dynamic_slice_in_dim(vector, rank * share, share, 0)


def as_rows(values, multiple):
    pad = -values.shape[-1] % (128 * multiple)
    values = jnp.pad(values, [(0, 0)] * (values.ndim - 1) + [(0, pad)])
    return values.reshape(*values.shape[:-1], -1, 128)


def call(kernel, number, out_shape, scratch, bytes_moved, *operands):
    vmem = pl.BlockSpec(memory_space=pltpu.VMEM)
    return pl.pallas_call(
        kernel,
        out_shape=out_shape,
        in_specs=[vmem] * len(operands),
        out_specs=jax.tree.map(lambda _: vmem, out_shape),
        scratch_shapes=scratch,
        compiler_params=pltpu.CompilerParams(
            collective_id=number, has_side_effects=True, vmem_limit_bytes=40 * 2**20
        ),
        cost_estimate=pl.CostEstimate(flops=0, bytes_accessed=bytes_moved, transcendentals=0),
    )(*operands)


def greet(peers):
    barrier = pltpu.get_barrier_semaphore()
    for peer in peers:
        pl.semaphore_signal(barrier, inc=1, device_id=peer, device_id_type=pl.DeviceIdType.MESH)
    pl.semaphore_wait(barrier, len(peers))


def send(source, target, sems, slot, peer):
    return pltpu.make_async_remote_copy(
        src_ref=source,
        dst_ref=target,
        send_sem=sems[0].at[slot],
        recv_sem=sems[1].at[slot],
        device_id=peer,
        device_id_type=pl.DeviceIdType.MESH,
    )


def peers_along(axis, n):
    me = lax.axis_index(axis)
    return [{axis: lax.rem(me + step, n)} for step in range(1, n)]


def block(ref, index, rows):
    return ref.at[pl.ds(pl.multiple_of(index * rows, 16), rows)]


def gather_kernel(n, x, out, *sems):
    rows = x.shape[0]
    me = lax.axis_index("tensor")
    peers = peers_along("tensor", n)
    greet(peers)
    copies = [
        send(x, block(out, me, rows), sems, step, peer) for step, peer in enumerate(peers)
    ]
    for copy in copies:
        copy.start()
    block(out, me, rows)[...] = x[...]
    for copy in copies:
        copy.wait()


def gather(x, number):
    n = lax.axis_size("tensor")
    shape = jax.ShapeDtypeStruct((n * x.shape[0], x.shape[1]), x.dtype)
    sems = [pltpu.SemaphoreType.DMA((n - 1,))] * 2
    return call(partial(gather_kernel, n), number, shape, sems, 2**24, x)


def scatter_start(n, x, held, sems, peers):
    rows = x.shape[0] // n
    me = lax.axis_index("tensor")
    copies = [
        send(block(x, lax.rem(me + step + 1, n), rows), held.at[step], sems, step, peer)
        for step, peer in enumerate(peers)
    ]
    for copy in copies:
        copy.start()
    return copies


def scatter_end(n, x, out, held, copies):
    rows = x.shape[0] // n
    total = block(x, lax.axis_index("tensor"), rows)[...].astype(jnp.float32)
    for step, copy in enumerate(copies):
        copy.wait_recv()
        total += held[step].astype(jnp.float32)
    out[...] = total
    for copy in copies:
        copy.wait_send()


def scatter_kernel(n, x, out, held, *sems):
    peers = peers_along("tensor", n)
    greet(peers)
    scatter_end(n, x, out, held, scatter_start(n, x, held, sems, peers))


def scatter(terms, number):
    n = lax.axis_size("tensor")
    rows, width = terms.shape[0] // n, terms.shape[1]
    return call(
        partial(scatter_kernel, n),
        number,
        jax.ShapeDtypeStruct((rows, width), jnp.float32),
        [pltpu.VMEM((n - 1, rows, width), jnp.bfloat16)] + [pltpu.SemaphoreType.DMA((n - 1,))] * 2,
        2**24,
        terms.astype(jnp.bfloat16),
    )


def line_gather_kernel(n, x, out, *sems):
    rows = x.shape[0]
    me = lax.axis_index("seq")
    greet(peers_along("seq", n))
    right, left = {"seq": lax.rem(me + 1, n)}, {"seq": lax.rem(me + n - 1, n)}
    block(out, me, rows)[...] = x[...]

    def hop(step, side):
        owner = lax.rem(me + (n - step if side == 0 else step), n)
        here = block(out, owner, rows)
        return send(here, here, sems[2 * side : 2 * side + 2], step, (right, left)[side])

    for step in range(n - 1):
        pl.when((me >= step) & (me < n - 1))(lambda: hop(step, 0).start())
        pl.when((me + step < n) & (me > 0))(lambda: hop(step, 1).start())
        pl.when(me > step)(lambda: hop(step, 0).wait_recv())
        pl.when(me + step + 1 < n)(lambda: hop(step, 1).wait_recv())
    for step in range(n - 1):
        pl.when((me >= step) & (me < n - 1))(lambda: hop(step, 0).wait_send())
        pl.when((me + step < n) & (me > 0))(lambda: hop(step, 1).wait_send())


def line_gather(x, number):
    n = lax.axis_size("seq")
    shape = jax.ShapeDtypeStruct((n * x.shape[0], x.shape[1]), x.dtype)
    sems = [pltpu.SemaphoreType.DMA((n - 1,))] * 4
    return call(partial(line_gather_kernel, n), number, shape, sems, 2**25, x)


def line_scatter_kernel(n, x, out, held, staged, *sems):
    rows = x.shape[0] // n
    me = lax.axis_index("seq")
    greet(peers_along("seq", n))
    neighbours = {"seq": lax.rem(me + 1, n)}, {"seq": lax.rem(me + n - 1, n)}

    def hop(step, side):
        return send(
            staged.at[side, step],
            held.at[side, step],
            sems[2 * side : 2 * side + 2],
            step,
            neighbours[side],
        )

    def advance(step, side):
        place = me if side == 0 else n - 1 - me
        mine = x[pl.ds((n - 1 - step if side == 0 else step) * rows, rows), :]

        def first():
            staged[side, step] = mine
            hop(step, side).start()

        def later():
            passing = held[side, step].astype(jnp.float32)
            staged[side, step] = (mine.astype(jnp.float32) + passing).astype(mine.dtype)
            hop(step, side).start()

        pl.when((place > 0) & (place <= n - 1 - step))(lambda: hop(step, side).wait_recv())
        pl.when(place == 0)(first)
        pl.when((place > 0) & (place < n - 1 - step))(later)

    for step in range(n - 1):
        advance(step, 0)
        advance(step, 1)
    out[...] = block(x, me, rows)[...].astype(jnp.float32)

    def add(side, step):
        out[...] += held[side, step].astype(jnp.float32)

    for step in range(n - 1):
        pl.when(me == n - 1 - step)(lambda: add(0, step))
        pl.when(me == step)(lambda: add(1, step))
    for step in range(n - 1):
        pl.when(me < n - 1 - step)(lambda: hop(step, 0).wait_send())
        pl.when(n - 1 - me < n - 1 - step)(lambda: hop(step, 1).wait_send())


def line_scatter(x, number):
    n = lax.axis_size("seq")
    rows, width = x.shape[0] // n, x.shape[1]
    return call(
        partial(line_scatter_kernel, n),
        number,
        jax.ShapeDtypeStruct((rows, width), jnp.float32),
        [pltpu.VMEM((2, n - 1, rows, width), x.dtype)] * 2
        + [pltpu.SemaphoreType.DMA((n - 1,))] * 4,
        2**25,
        x,
    )


def final_kernel(
    n,
    dp,
    seq,
    term,
    mlp,
    w,
    v_one,
    v_two,
    early,
    term_out,
    mlp_out,
    w_out,
    v_out,
    early_out,
    term_held,
    mlp_held,
    w_held,
    w_total,
    v_one_held,
    v_mine,
    v_held,
    *sems,
):
    f32 = jnp.float32
    count = dp * seq
    rows = w.shape[0] // count
    lane = lax.axis_index("tensor")
    me = lax.axis_index("dp") * seq + lax.axis_index("seq")
    near = peers_along("tensor", n)

    def far(step):
        index = lax.rem(me + step, count)
        return index, {"dp": index // seq, "seq": lax.rem(index, seq)}

    barrier = pltpu.get_barrier_semaphore()

    def signal(peer):
        pl.semaphore_signal(barrier, inc=1, device_id=peer, device_id_type=pl.DeviceIdType.MESH)

    for peer in near:
        signal(peer)
    pl.loop(1, count)(lambda step: signal(far(step)[1]))
    pl.semaphore_wait(barrier, n - 1 + count - 1)

    pairs = [sems[i : i + 2] for i in range(0, len(sems), 2)]
    ones = [
        send(v_one.at[lax.rem(lane + step + 1, n)], v_one_held.at[step], pairs[0], step, peer)
        for step, peer in enumerate(near)
    ]
    for copy in ones:
        copy.start()

    def first(step):
        index, peer = far(step)
        return send(block(w, index, rows), w_held.at[step - 1], pairs[1], step - 1, peer)

    def second(step):
        here = block(w_out, me, rows)
        return send(here, here, pairs[2], step - 1, far(step)[1])

    def spread(step):
        return send(early, block(early_out, me, early.shape[0]), pairs[6], step - 1, far(step)[1])

    def vector(step):
        return send(v_mine, v_held.at[step - 1], pairs[3], step - 1, far(step)[1])

    pl.loop(1, count)(lambda step: first(step).start())
    terms = scatter_start(n, term, term_held, pairs[4], near)
    mlps = scatter_start(n, mlp, mlp_held, pairs[5], near)
    total = v_one[lane]
    for step, copy in enumerate(ones):
        copy.wait_recv()
        total += v_one_held[step]
    v_mine[0:8, :] = total
    v_mine[8:, :] = v_two[...]
    pl.loop(1, count)(lambda step: vector(step).start())
    pl.loop(1, count)(lambda step: spread(step).start())
    block(early_out, me, early.shape[0])[...] = early[...]
    w_total[...] = block(w, me, rows)[...].astype(f32)

    @pl.loop(1, count)
    def _(step):
        first(step).wait_recv()
        w_total[...] += w_held[step - 1].astype(f32)

    block(w_out, me, rows)[...] = w_total[...].astype(w_out.dtype)
    pl.loop(1, count)(lambda step: second(step).start())
    scatter_end(n, term, term_out, term_held, terms)
    scatter_end(n, mlp, mlp_out, mlp_held, mlps)
    v_out[...] = v_mine[...]

    @pl.loop(1, count)
    def _(step):
        vector(step).wait_recv()
        v_out[...] += v_held[step - 1]

    for copy in ones:
        copy.wait_send()

    @pl.loop(1, count)
    def _(step):
        second(step).wait_recv()
        first(step).wait_send()
        second(step).wait_send()
        vector(step).wait_send()
        spread(step).wait_recv()
        spread(step).wait_send()


def padded(w, count):
    pad = -w.shape[0] % (16 * count)
    return jnp.pad(w, ((0, pad), (0, 0))) if pad else w


def final(term, mlp, w, v_one, v_two, early, number):
    n, dp, seq = lax.axis_size("tensor"), lax.axis_size("dp"), lax.axis_size("seq")
    f32, bf16 = jnp.float32, jnp.bfloat16
    count = dp * seq
    w = padded(w, count)
    rows = term.shape[0] // n
    vectors = (8 + v_two.shape[0], 128)
    part = w.shape[0] // count
    held = pltpu.VMEM((n - 1, rows, term.shape[1]), bf16)
    near, far = [pltpu.SemaphoreType.DMA((n - 1,))] * 2, [pltpu.SemaphoreType.DMA((count - 1,))] * 2
    return call(
        partial(final_kernel, n, dp, seq),
        number,
        (
            jax.ShapeDtypeStruct((rows, term.shape[1]), f32),
            jax.ShapeDtypeStruct((rows, term.shape[1]), f32),
            jax.ShapeDtypeStruct(w.shape, bf16),
            jax.ShapeDtypeStruct(vectors, f32),
            jax.ShapeDtypeStruct((count * early.shape[0], early.shape[1]), bf16),
        ),
        [
            held,
            held,
            pltpu.VMEM((count - 1, part, w.shape[1]), bf16),
            pltpu.VMEM((part, w.shape[1]), f32),
            pltpu.VMEM((n - 1, 8, 128), f32),
            pltpu.VMEM(vectors, f32),
            pltpu.VMEM((count - 1, *vectors), f32),
        ]
        + near
        + far * 3
        + near * 2
        + far,
        2**26,
        term,
        mlp,
        w,
        v_one,
        v_two,
        early,
    )


def local(
    inputs,
    ln1_gain,
    ln1_bias,
    w_query,
    b_query,
    w_key,
    w_value,
    b_value,
    w_out,
    b_out,
    ln2_gain,
    ln2_bias,
    w_up,
    b_up,
    w_down,
    b_down,
    cotangent,
):
    f32, bf16 = jnp.float32, jnp.bfloat16
    own_rows, width = inputs.shape[1:]
    lanes = lax.axis_size("tensor")
    rank = lax.axis_index("tensor")
    share = width // lanes
    gain_one = ln1_gain.astype(f32)
    gain_two = ln2_gain.astype(f32)
    frames_in = inputs[0].astype(f32)
    both = gather(jnp.concatenate([inputs[0], cotangent[0]], axis=1), 1)
    grad_z_all = both[:, width:]
    normed_one, scaled_all, _ = normalize(
        both[:, :width].astype(f32), gain_one, ln1_bias.astype(f32)
    )
    attn_input = normed_one.astype(bf16)
    heads_width = w_query.shape[1]
    keys = product(attn_input, w_key).astype(bf16)
    values = (product(attn_input, w_value) + b_value.astype(f32)).astype(bf16)
    kv_all = line_gather(jnp.concatenate([keys, values], axis=1), 2)
    query = (product(attn_input, w_query) + b_query.astype(f32)).astype(bf16)
    grad_hidden = product_cols(grad_z_all, w_down)
    frames = query.shape[0]
    heads = heads_width // HEAD_DIM
    scale = HEAD_DIM ** (-0.5)
    query3 = query.reshape(frames, heads, HEAD_DIM)
    key3 = kv_all[:, :heads_width].reshape(kv_all.shape[0], heads, HEAD_DIM)
    value3 = kv_all[:, heads_width:].reshape(kv_all.shape[0], heads, HEAD_DIM)
    scores = jnp.einsum("qhd,khd->hqk", query3, key3, preferred_element_type=f32) * scale
    top = jnp.max(scores, axis=-1, keepdims=True)
    expo = jnp.exp(scores - top)
    total = jnp.sum(expo, axis=-1, keepdims=True)
    logsum = top + jnp.log(total)
    weights_low = (expo / total).astype(bf16)
    context = jnp.einsum("hqk,khd->qhd", weights_low, value3, preferred_element_type=f32)
    context = context.reshape(frames, heads_width).astype(bf16)
    attn_rows = scatter(product(context, w_out), 3)
    middle = frames_in + attn_rows + b_out.astype(f32)
    normed_two, scaled_two, spread_two = normalize(middle, gain_two, ln2_bias.astype(f32))
    mlp_input = gather(normed_two.astype(bf16), 4)
    before = product(mlp_input, w_up) + b_up.astype(f32)
    activated, gelu_back = jax.vjp(partial(jax.nn.gelu, approximate=False), before)
    hidden = activated.astype(bf16)
    (grad_before,) = gelu_back(grad_hidden)
    grad_before = grad_before.astype(bf16)
    grad_two = scatter(product_cols(grad_before, w_up), 5)
    upstream = cotangent[0].astype(f32)
    grad_middle = upstream + normalize_back(grad_two, scaled_two, spread_two, gain_two)
    grad_attn_rows = grad_middle.astype(bf16)
    sums_two = jnp.stack([jnp.sum(grad_two * scaled_two, axis=0), jnp.sum(grad_two, axis=0)])
    high = sums_two.astype(bf16)
    low = (sums_two - high.astype(f32)).astype(bf16)
    extra = jnp.concatenate([high, low, jnp.zeros((12, width), bf16)])
    packed = gather(jnp.concatenate([grad_attn_rows, extra]), 6).reshape(lanes, -1, width)
    grad_attn_all = packed[:, :own_rows].reshape(frames, width)
    pair = packed[:, own_rows : own_rows + 4].astype(f32).sum(axis=0)
    pair = lax.dynamic_slice_in_dim(pair[:2] + pair[2:], rank * share, share, 1)
    mlp_terms = product(hidden, w_down).astype(bf16)
    grad_down = product_rows(hidden, grad_z_all)
    grad_up = product_rows(mlp_input, grad_before)
    early = padded(
        jnp.concatenate([grad_up.astype(bf16), grad_down.astype(bf16)], axis=1),
        lax.axis_size("dp") * lax.axis_size("seq"),
    )
    early = lax.psum_scatter(early, ("dp", "seq"), scatter_dimension=0, tiled=True)
    grad_wout = product_rows(grad_attn_all, context)
    grad_context = (
        product_cols(grad_attn_all, w_out).astype(bf16).reshape(frames, heads, HEAD_DIM)
    )
    scores_again = jnp.einsum("qhd,khd->hqk", query3, key3, preferred_element_type=f32) * scale
    probs = jnp.exp(scores_again - logsum)
    probs_low = probs.astype(bf16)
    grad_probs = jnp.einsum("qhd,khd->hqk", grad_context, value3, preferred_element_type=f32)
    inner_sum = jnp.sum(probs * grad_probs, axis=-1, keepdims=True)
    grad_scores = (probs * (grad_probs - inner_sum)).astype(bf16)
    key_terms = jnp.einsum("hqk,qhd->khd", grad_scores, query3, preferred_element_type=f32) * scale
    key_terms = key_terms.reshape(kv_all.shape[0], heads_width)
    value_terms = jnp.einsum("hqk,qhd->khd", probs_low, grad_context, preferred_element_type=f32)
    value_terms = value_terms.reshape(kv_all.shape[0], heads_width)
    grad_kv = line_scatter(
        jnp.concatenate([key_terms, value_terms], axis=1).astype(bf16), 7
    ).astype(bf16)
    grad_query = jnp.einsum("hqk,khd->qhd", grad_scores, key3, preferred_element_type=f32) * scale
    grad_query = grad_query.reshape(frames, heads_width).astype(bf16)
    grad_keys = grad_kv[:, :heads_width]
    grad_values = grad_kv[:, heads_width:]
    term = (
        product_cols(grad_query, w_query)
        + product_cols(grad_keys, w_key)
        + product_cols(grad_values, w_value)
    )
    grad_qkv = product_rows(attn_input, jnp.concatenate([grad_query, grad_kv], axis=1))
    sums_one = jnp.stack([jnp.sum(term * scaled_all, axis=0), jnp.sum(term, axis=0)])
    v_one = sums_one.reshape(2, lanes, share).swapaxes(0, 1).reshape(lanes, -1)
    v_one = as_rows(v_one, 8)
    mine = [
        jnp.sum(grad_query.astype(f32), axis=0),
        jnp.sum(grad_values.astype(f32), axis=0),
        own_columns(jnp.sum(grad_attn_all.astype(f32), axis=0), rank, share),
        pair[0],
        pair[1],
        own_columns(jnp.sum(grad_z_all.astype(f32), axis=0), rank, share),
        jnp.sum(grad_before.astype(f32), axis=0),
    ]
    ends = np.cumsum([part.shape[0] for part in mine])
    grad_one, mlp_rows, late, totals, early = final(
        term.astype(bf16),
        mlp_terms,
        jnp.concatenate([grad_qkv.astype(bf16), grad_wout.astype(bf16)], axis=1),
        v_one,
        as_rows(jnp.concatenate(mine), 16),
        early,
        8,
    )
    result = (middle + mlp_rows + b_down.astype(f32)).astype(bf16)
    late = late[:width].astype(f32)
    gain1, bias1 = totals[:8].reshape(-1)[: 2 * share].reshape(2, share)
    bq, bv, bo, gain2, bias2, bd, bu = jnp.split(totals[8:].reshape(-1)[: ends[-1]], ends[:-1])
    scaled_one, spread_one = normalize(frames_in, gain_one, ln1_bias.astype(f32))[1:]
    grad_input = (grad_middle + normalize_back(grad_one, scaled_one, spread_one, gain_one)).astype(
        bf16
    )
    return (
        result[None],
        grad_input[None],
        gain1,
        bias1,
        late[:, :heads_width],
        bq,
        late[:, heads_width : 2 * heads_width],
        late[:, 2 * heads_width : 3 * heads_width],
        bv,
        late[:, 3 * heads_width :].T,
        bo,
        gain2,
        bias2,
        early[:width, : b_up.shape[0]].astype(f32),
        bu,
        early[:width, b_up.shape[0] :].astype(f32),
        bd,
    )


def solution(mesh):
    placed = (
        P("dp", ("seq", "tensor"), None),
        P(),
        P(),
        P(None, "tensor"),
        P("tensor"),
        P(None, "tensor"),
        P(None, "tensor"),
        P("tensor"),
        P("tensor", None),
        P(),
        P(),
        P(),
        P(None, "tensor"),
        P("tensor"),
        P("tensor", None),
        P(),
        P("dp", ("seq", "tensor"), None),
    )
    return jax.shard_map(
        local,
        mesh=mesh,
        in_specs=placed,
        out_specs=(
            P("dp", ("seq", "tensor"), None),
            P("dp", ("seq", "tensor"), None),
            P("tensor"),
            P("tensor"),
            P(None, "tensor"),
            P("tensor"),
            P(None, "tensor"),
            P(None, "tensor"),
            P("tensor"),
            P("tensor", None),
            P("tensor"),
            P("tensor"),
            P("tensor"),
            P(None, "tensor"),
            P("tensor"),
            P("tensor", None),
            P("tensor"),
        ),
        check_vma=False,
    )
```
